32 devices in a mesh: groups: 2 (over y), space: 4 (over z), tm: 2 (over x), obs: 2 (over core).
Axes of the slice: x: 2, y: 2, z: 4, core: 2. Of those that a mesh axis runs over, the one named last changes fastest.
Arguments:
- state: bfloat16 [2048, 16384], P(('groups', 'tm', 'obs'), 'space'), parts along dimension 0, may hold values from -6 to 6
- spatial_factor: bfloat16 [16384, 16384], P(('tm', 'obs'), 'space'), may hold values from -0.0625 to 0.0625
- time_factor: bfloat16 [1024, 1024], P('space'), as said below
- footprints: bfloat16 [64, 48, 2048], P(('groups', 'space'), None, ('tm', 'obs')), parts along dimension 0, may hold values from -0.0390625 to 0.0390625
- tile_obs: int32 [64, 4], P(('groups', 'space'), ('tm', 'obs')), parts along dimension 0, may hold values from 0 to 31
- tile_block: int32 [64, 4], P(('groups', 'space'), ('tm', 'obs')), parts along dimension 0, may hold values from 0 to 7
- tile_hour: int32 [64, 4], P(('groups', 'space'), ('tm', 'obs')), parts along dimension 0, may hold values from 0 to 976, as said below
- tile_count: int32 [8, 4], P(('groups', 'space'), ('tm', 'obs')), parts along dimension 0, may hold values from 1 to 8, as said below
- obs_weight: float32 [64], P('groups'), parts along dimension 0, may hold values from 10 to 100
Outputs:
- hessian_product: float32 [2048, 16384], P(('groups', 'tm', 'obs'), 'space'), parts along dimension 0
The draws below stay inside these ranges and needn't reach their ends.
There are 2 independent parts, one for each index of `groups`. The reference program is written for one: setup_inputs(seed, part) draws one part's arguments, and reference() takes and returns one part's arrays. A program takes and returns all parts, laid end to end along the dimension named above; an argument that names none is the same for every part. Nothing has to cross between parts.
Inputs may be any that keep to these rules, and one draw needn't show every extreme that they name: time_factor is symmetric. `tile_hour`: the tiles of row r start in the block of hours r // 8, hours (r // 8) * 256 to (r // 8) * 256 + 255. `tile_count`: the live slots are the first ones of each owner and block of hours; some entry equals 8.
All inputs are finite; a program needn't handle non-finite values.
Results may differ from the reference program's by a relative error of at most 0.019.
Values may be sent and summed in bfloat16 or wider, within the bound.
A program may use at most 128 MiB of HBM per device.

```python
import math
import jax
import jax.numpy as jnp
from jax import lax

CELLS = 16384
HOURS = 1024
LAGS = 48
CB = 512
SLOTS = 8
HOUR_BLOCKS = 4
OWNERS = 4
HB = 256
CELL_ROWS = 4096
TILE_ROWS = 32
TILE_COLS = 2048
NOBS = 32
N_SPACE = 4
N_TM = 2
N_OBS = 2


def draw_time_factor(key, part):
    first, second = jax.random.split(key, 2)
    base = jax.random.normal(first, (HOURS, HOURS), jnp.float32)
    matrix = (base + base.T) * (0.6 / math.sqrt(2.0 * HOURS))
    diagonal_values = jax.random.uniform(second, (HOURS,), jnp.float32, 0.8, 1.2)
    identity = (lax.broadcasted_iota(jnp.int32, (HOURS, HOURS), 0) == lax.broadcasted_iota(jnp.int32, (HOURS, HOURS), 1)).astype(jnp.float32)
    matrix = matrix + identity * diagonal_values[None, :]
    return matrix.astype(jnp.bfloat16)


def draw_tile_hour(key, part):
    row_index = lax.broadcasted_iota(jnp.int32, (TILE_ROWS, OWNERS), 0)
    owner_index = lax.broadcasted_iota(jnp.int32, (TILE_ROWS, OWNERS), 1)
    block = row_index // SLOTS
    raw = jax.random.randint(key, (TILE_ROWS, OWNERS), 0, 1 << 20)
    half_lags = LAGS // 2
    late_hour = block * HB + HB - half_lags + raw % half_lags
    last_limit = HOURS - LAGS + 1 - block * HB
    last_hour = block * HB + raw % jnp.maximum(last_limit, 1)
    hour = jnp.where(block == HOUR_BLOCKS - 1, last_hour, late_hour)
    hour = jnp.where((row_index == 0) & (owner_index == 0), 0, hour)
    hour = jnp.where((row_index == TILE_ROWS - SLOTS) & (owner_index == 0), HOURS - LAGS, hour)
    return hour.astype(jnp.int32)


def draw_tile_count(key, part):
    first, second, third = jax.random.split(jax.random.fold_in(key, 7), 3)
    left = jax.random.randint(first, (HOUR_BLOCKS, OWNERS), 0, SLOTS)
    right = jax.random.randint(second, (HOUR_BLOCKS, OWNERS), 0, SLOTS)
    count = 1 + left * (right + SLOTS) // (2 * SLOTS)
    chosen = jax.random.randint(third, (), 0, HOUR_BLOCKS * OWNERS)
    flat_index = lax.broadcasted_iota(jnp.int32, (HOUR_BLOCKS, OWNERS), 0) * OWNERS + lax.broadcasted_iota(jnp.int32, (HOUR_BLOCKS, OWNERS), 1)
    count = jnp.where(flat_index == chosen, SLOTS, count)
    return count.astype(jnp.int32)


def set_ends(entries, own_key, smallest, high):
    spot = [jax.random.randint(jax.random.fold_in(own_key, axis), (), 0, length) for axis, length in enumerate(entries.shape)]
    longest = entries.shape.index(max(entries.shape))
    next_to = spot[:longest] + [(spot[longest] + 1) % entries.shape[longest]] + spot[longest + 1:]
    return entries.at[tuple(spot)].set(smallest).at[tuple(next_to)].set(high)


def with_spikes(array, key, source, target, shards_of, factor):
    def block_of(axis_at):
        return (jnp.arange(array.shape[axis_at]) // (array.shape[axis_at] // shards_of)).reshape((-1,) + (1,) * (array.ndim - 1 - axis_at))

    first = jax.random.permutation(key, shards_of)[block_of(target)]
    far = (block_of(target) + shards_of // 2) % shards_of
    return jnp.where((block_of(source) == first) | (block_of(source) == far), factor * array, array)


def block_levels(rng, shape, cuts, low, high):
    def one(axis_at, blocks):
        steps = jax.random.uniform(jax.random.fold_in(jax.random.fold_in(rng, 6), axis_at), (blocks,), jnp.float32, low / len(cuts), high / len(cuts))
        return jnp.repeat(jnp.exp(steps), shape[axis_at] // blocks).reshape((-1,) + (1,) * (len(shape) - axis_at - 1))

    gain = one(*cuts[0])
    for cut in cuts[1:]:
        gain = gain * one(*cut)
    return gain


def noise(own_key, dims, scale, limit, shards=(), kind=jnp.bfloat16):
    values = jax.random.normal(own_key, dims, jnp.float32) * scale
    if len(shards) > 0:
        values = block_levels(own_key, dims, shards, -0.22, 0.18) * values
    return jnp.clip(values, min=-limit, max=limit).astype(kind)


def heavy_noise(rng, extent, width, limit, shards, heavy, kind=jnp.bfloat16):
    result = width * jax.random.normal(rng, extent, jnp.float32)
    if shards:
        result = result * block_levels(rng, extent, shards, -0.22, 0.18)
    return jnp.clip(with_spikes(result, jax.random.fold_in(rng, 3), *heavy), -limit, limit).astype(kind)


def setup_inputs(seed: int = 0, part: int = 0) -> dict:
    key_of = jax.random.split(jax.random.key(seed), 10)
    part_keys = jax.random.split(jax.random.fold_in(key_of[9], part), 10)
    return {
        "state": noise(part_keys[0], (HOURS, CELLS), 1.0, 6.0, ((0, 4), (1, 4))),
        "spatial_factor": heavy_noise(key_of[1], (CELLS, CELLS), CELLS ** -0.5, 0.0625, ((0, 4), (1, 4)), (0, 1, 4, 2.0)),
        "time_factor": draw_time_factor(jax.random.fold_in(key_of[9], 71), part),
        "footprints": noise(part_keys[3], (TILE_ROWS, LAGS, TILE_COLS), (LAGS * CB) ** -0.5, 0.0390625, ((0, 4), (2, 4))),
        "tile_obs": set_ends(jax.random.randint(part_keys[4], (TILE_ROWS, OWNERS), 0, NOBS), jax.random.fold_in(part_keys[4], 1), 0, NOBS - 1).astype(jnp.int32),
        "tile_block": set_ends(jax.random.randint(part_keys[5], (TILE_ROWS, OWNERS), 0, CELL_ROWS // CB), jax.random.fold_in(part_keys[5], 1), 0, (CELL_ROWS // CB) - 1).astype(jnp.int32),
        "tile_hour": draw_tile_hour(jax.random.fold_in(jax.random.fold_in(key_of[9], part), 71), part),
        "tile_count": draw_tile_count(jax.random.fold_in(jax.random.fold_in(key_of[9], part), 71), part),
        "obs_weight": jnp.clip(jnp.exp(jax.random.uniform(part_keys[8], (NOBS,), jnp.float32, math.log(10.0), math.log(100.0))), 10.0, 100.0),
    }


def reference(state, spatial_factor, time_factor, footprints, tile_obs, tile_block, tile_hour, tile_count, obs_weight):
    cell_cols = CELLS // N_SPACE
    owners = N_TM * N_OBS
    cell_rows = CELLS // owners

    def forward_block(total, index):
        begin = index * cell_cols
        part_state = lax.dynamic_slice_in_dim(state, begin, cell_cols, 1)
        part_factor = lax.dynamic_slice_in_dim(spatial_factor, begin, cell_cols, 1)
        term = lax.dot_general(part_state, part_factor, (((1,), (1,)), ((), ())), preferred_element_type=jnp.float32)
        term = lax.optimization_barrier(term.astype(jnp.bfloat16)).astype(jnp.float32)
        return total + term, None

    summed, _ = lax.scan(forward_block, jnp.zeros((HOURS, CELLS), jnp.float32), jnp.arange(N_SPACE, dtype=jnp.int32))
    mixed = summed.astype(jnp.bfloat16)
    field = jnp.dot(time_factor, mixed, preferred_element_type=jnp.float32).astype(jnp.bfloat16)

    row_index = lax.broadcasted_iota(jnp.int32, (TILE_ROWS, owners), 0)
    owner_index = lax.broadcasted_iota(jnp.int32, (TILE_ROWS, owners), 1)
    limits = tile_count[row_index // SLOTS, owner_index]
    live_flat = (row_index % SLOTS < limits).reshape(-1).astype(jnp.float32)
    hours_flat = tile_hour.reshape(-1).astype(jnp.int32)
    corner_flat = (owner_index * cell_rows + tile_block * CB).reshape(-1).astype(jnp.int32)
    tiles = footprints.reshape(TILE_ROWS, LAGS, owners, CB).transpose(0, 2, 1, 3).reshape(-1, LAGS, CB)
    obs_flat = tile_obs.reshape(-1)

    def measure(item):
        hour, corner, tile = item
        window = lax.dynamic_slice(field, (hour, corner), (LAGS, CB))
        return jnp.sum(window.astype(jnp.float32) * tile.astype(jnp.float32))

    modeled = lax.map(measure, (hours_flat, corner_flat, tiles)) * live_flat
    totals = jax.ops.segment_sum(modeled, obs_flat, num_segments=NOBS)
    innovation = obs_weight * totals
    weights = innovation[obs_flat] * live_flat

    def deposit(grid, item):
        hour, corner, tile, weight = item
        push = (weight * tile.astype(jnp.float32)).astype(jnp.bfloat16)
        push = lax.optimization_barrier(push).astype(jnp.float32)
        here = lax.dynamic_slice(grid, (hour, corner), (LAGS, CB))
        return lax.dynamic_update_slice(grid, here + push, (hour, corner)), None

    grid, _ = lax.scan(deposit, jnp.zeros((HOURS, CELLS), jnp.float32), (hours_flat, corner_flat, tiles, weights))
    adjoint_field = grid.astype(jnp.bfloat16)
    back_time = jnp.dot(time_factor.T, adjoint_field, preferred_element_type=jnp.float32).astype(jnp.bfloat16)

    def adjoint_block(total, index):
        begin = index * cell_rows
        part_back = lax.dynamic_slice_in_dim(back_time, begin, cell_rows, 1)
        part_factor = lax.dynamic_slice_in_dim(spatial_factor, begin, cell_rows, 0)
        term = jnp.dot(part_back, part_factor, preferred_element_type=jnp.float32)
        term = lax.optimization_barrier(term.astype(jnp.bfloat16)).astype(jnp.float32)
        return total + term, None

    spread, _ = lax.scan(adjoint_block, jnp.zeros((HOURS, CELLS), jnp.float32), jnp.arange(owners, dtype=jnp.int32))
    return state.astype(jnp.float32) + spread
```

```python
import functools

import jax
import jax.numpy as jnp
from jax import lax
from jax.experimental import pallas as pl
from jax.experimental.pallas import tpu as pltpu
from jax.sharding import PartitionSpec as P

ALIGN = 16
GROUP = 4


def chunk_of(columns, most):
    chunk = min(columns, most)
    while columns % chunk:
        chunk //= 2
    return chunk


def image_kernel(lags, rows, step, order_ref, shift_ref, start_ref, tiles_ref, factor_ref, image_ref, held):
    block = pl.program_id(0)
    begin, end = start_ref[block], start_ref[block + 1]
    last = order_ref.shape[0] - 1
    width = tiles_ref.shape[2]
    columns = factor_ref.shape[1]

    def group(index, carry):
        first = begin + index * GROUP
        for k in range(GROUP):
            at = jnp.minimum(first + k, last)
            tile = tiles_ref[order_ref[at]].astype(jnp.float32)
            tile = jnp.concatenate([tile, jnp.zeros((rows - lags, width), jnp.float32)], axis=0)
            tile = pltpu.roll(tile, shift_ref[at], 0)
            held[k * rows : (k + 1) * rows, :] = tile.astype(jnp.bfloat16)

        def part(piece, inner):
            span = pl.ds(pl.multiple_of(piece * step, step), step)
            product = jnp.dot(held[...], factor_ref[:, span], preferred_element_type=jnp.float32)
            product = product.astype(jnp.bfloat16)
            for k in range(GROUP):

                @pl.when(first + k < end)
                def _():
                    image_ref[first + k, :, span] = product[k * rows : (k + 1) * rows]

            return inner

        lax.fori_loop(0, columns // step, part, 0)
        return carry

    lax.fori_loop(0, (end - begin + GROUP - 1) // GROUP, group, 0)


def images(order, shift, start, tiles, factor, rows):
    count, lags, width = tiles.shape
    cells, columns = factor.shape
    step = chunk_of(columns, 1024)
    return pl.pallas_call(
        functools.partial(image_kernel, lags, rows, step),
        grid_spec=pltpu.PrefetchScalarGridSpec(
            num_scalar_prefetch=3,
            grid=(cells // width,),
            in_specs=[
                pl.BlockSpec((count, lags, width), lambda i, *_: (0, 0, 0)),
                pl.BlockSpec((width, columns), lambda i, *_: (i, 0)),
            ],
            out_specs=pl.BlockSpec((count, rows, columns), lambda i, *_: (0, 0, 0)),
            scratch_shapes=[pltpu.VMEM((GROUP * rows, width), jnp.bfloat16)],
        ),
        out_shape=jax.ShapeDtypeStruct((count, rows, columns), jnp.bfloat16),
        compiler_params=pltpu.CompilerParams(vmem_limit_bytes=58 * 1024 * 1024),
        cost_estimate=pl.CostEstimate(
            flops=2 * count * rows * width * columns, bytes_accessed=2 * cells * columns, transcendentals=0
        ),
        name="images",
    )(order, shift, start, tiles, factor)


def window_kernel(rows, base_ref, live_ref, factor_ref, state_ref, image_ref, sums_ref, field):
    @pl.when(pl.program_id(0) == 0)
    def _():
        sums_ref[...] = jnp.zeros_like(sums_ref)

    field[...] = jnp.dot(factor_ref[...], state_ref[...], preferred_element_type=jnp.float32)
    columns = state_ref.shape[1]

    def one(at, carry):
        base = pl.multiple_of(base_ref[at], ALIGN)
        product = field[pl.ds(base, rows), :] * image_ref[at].astype(jnp.float32)
        product = jnp.sum(product.reshape(rows // 8, 8, columns), axis=0)
        total = product[:, :128]
        for k in range(1, columns // 128):
            total = total + product[:, k * 128 : (k + 1) * 128]
        sums_ref[at] += total
        return carry

    lax.fori_loop(0, live_ref[0], one, 0)


def window_sums(base, live, factor, state, image):
    hours, columns = state.shape
    count, rows, _ = image.shape
    step = chunk_of(columns, 512)
    return pl.pallas_call(
        functools.partial(window_kernel, rows),
        grid_spec=pltpu.PrefetchScalarGridSpec(
            num_scalar_prefetch=2,
            grid=(columns // step,),
            in_specs=[
                pl.BlockSpec((hours, hours), lambda i, *_: (0, 0)),
                pl.BlockSpec((hours, step), lambda i, *_: (0, i)),
                pl.BlockSpec((count, rows, step), lambda i, *_: (0, 0, i)),
            ],
            out_specs=pl.BlockSpec((count, 8, 128), lambda i, *_: (0, 0, 0)),
            scratch_shapes=[pltpu.VMEM((hours, step), jnp.float32)],
        ),
        out_shape=jax.ShapeDtypeStruct((count, 8, 128), jnp.float32),
        compiler_params=pltpu.CompilerParams(vmem_limit_bytes=58 * 1024 * 1024),
        name="window_sums",
    )(base, live, factor, state, image)


def back_kernel(rows, base_ref, live_ref, weight_ref, factor_ref, image_ref, out_ref, grid):
    grid[...] = jnp.zeros_like(grid)

    def one(at, carry):
        window = pl.ds(pl.multiple_of(base_ref[at], ALIGN), rows)
        grid[window, :] += weight_ref[at] * image_ref[at].astype(jnp.float32)
        return carry

    lax.fori_loop(0, live_ref[0], one, 0)
    out_ref[...] = lax.dot_general(
        factor_ref[...],
        grid[...].astype(jnp.bfloat16),
        (((1,), (0,)), ((), ())),
        preferred_element_type=jnp.float32,
    ).astype(jnp.bfloat16)


def back_product(base, live, weight, factor, image):
    hours = factor.shape[0]
    count, rows, columns = image.shape
    step = chunk_of(columns, 512)
    return pl.pallas_call(
        functools.partial(back_kernel, rows),
        grid_spec=pltpu.PrefetchScalarGridSpec(
            num_scalar_prefetch=3,
            grid=(columns // step,),
            in_specs=[
                pl.BlockSpec((hours, hours), lambda i, *_: (0, 0)),
                pl.BlockSpec((count, rows, step), lambda i, *_: (0, 0, i)),
            ],
            out_specs=pl.BlockSpec((hours, step), lambda i, *_: (0, i)),
            scratch_shapes=[pltpu.VMEM((hours, step), jnp.float32)],
        ),
        out_shape=jax.ShapeDtypeStruct((hours, columns), jnp.bfloat16),
        compiler_params=pltpu.CompilerParams(vmem_limit_bytes=58 * 1024 * 1024),
        name="back_product",
    )(base, live, weight, factor, image)


def per_device(
    state,
    spatial_factor,
    time_factor,
    footprints,
    tile_obs,
    tile_block,
    tile_hour,
    tile_count,
    obs_weight,
):
    slots, lags, width = footprints.shape
    blocks = spatial_factor.shape[0] // width
    observations = obs_weight.shape[0]
    rows = -(-lags // ALIGN) * ALIGN + ALIGN
    own_live = (jnp.arange(slots, dtype=jnp.int32)[:, None] < tile_count).astype(jnp.int32)
    table = lax.all_gather(
        jnp.concatenate([tile_obs, tile_block, tile_hour, own_live], axis=1), "space", axis=0, tiled=True
    )
    tiles = lax.all_gather(footprints, "space", axis=0, tiled=True)
    factor = lax.all_gather(time_factor, "space", axis=0, tiled=True)
    full_state = lax.all_gather(state, ("tm", "obs"), axis=0, tiled=True)
    hours = factor.shape[0]
    count = tiles.shape[0]

    key = jnp.where(table[:, 3] > 0, table[:, 1], blocks)
    number = jnp.arange(count, dtype=jnp.int32)
    before = (key[None, :] < key[:, None]) | ((key[None, :] == key[:, None]) & (number[None, :] < number[:, None]))
    rank = jnp.sum(before.astype(jnp.int32), axis=1)
    at_rank = (rank[None, :] == number[:, None]).astype(jnp.int32)
    order = jnp.sum(at_rank * number[None, :], axis=1)
    hour = jnp.sum(at_rank * table[:, 2][None, :], axis=1)
    obs = jnp.sum(at_rank * table[:, 0][None, :], axis=1)
    edges = jnp.arange(blocks + 1, dtype=jnp.int32)
    start = jnp.sum((key[None, :] < edges[:, None]).astype(jnp.int32), axis=1)
    live = start[blocks:]
    base = jnp.minimum(hour // ALIGN * ALIGN, hours - rows)
    shift = hour - base

    image = images(order, shift, start, tiles, spatial_factor, rows)
    sums = window_sums(base, live, factor, full_state, image)
    modeled = jnp.where(number < live, jnp.sum(sums, axis=(1, 2)), 0.0)
    onehot = obs[:, None] == jnp.arange(observations, dtype=jnp.int32)[None, :]
    local_totals = jnp.sum(jnp.where(onehot, modeled[:, None], 0.0), axis=0)
    innovation = obs_weight * lax.psum(local_totals, ("space", "tm", "obs"))
    weight = jnp.sum(jnp.where(onehot, innovation[None, :], 0.0), axis=1)
    spread = lax.psum_scatter(
        back_product(base, live, weight, factor, image), ("tm", "obs"), scatter_dimension=0, tiled=True
    )
    return state.astype(jnp.float32) + spread.astype(jnp.float32)


def solution(mesh):
    return jax.shard_map(
        per_device,
        mesh=mesh,
        in_specs=(
            P(("groups", "tm", "obs"), "space"),
            P(("tm", "obs"), "space"),
            P("space", None),
            P(("groups", "space"), None, ("tm", "obs")),
            P(("groups", "space"), ("tm", "obs")),
            P(("groups", "space"), ("tm", "obs")),
            P(("groups", "space"), ("tm", "obs")),
            P(("groups", "space"), ("tm", "obs")),
            P("groups"),
        ),
        out_specs=P(("groups", "tm", "obs"), "space"),
        check_vma=False,
    )
```

```python
import functools

import jax
import jax.numpy as jnp
from jax import lax
from jax.experimental import pallas as pl
from jax.experimental.pallas import tpu as pltpu
from jax.sharding import PartitionSpec as P

ALIGN = 16
GROUP = 4
MESH = pl.DeviceIdType.MESH


def chunk_of(columns, most):
    chunk = min(columns, most)
    while columns % chunk:
        chunk //= 2
    return chunk


def image_kernel(lags, rows, step, order_ref, shift_ref, start_ref, tiles_ref, factor_ref, image_ref, held):
    block = pl.program_id(0)
    begin, end = start_ref[block], start_ref[block + 1]
    last = order_ref.shape[0] - 1
    width = tiles_ref.shape[2]
    columns = factor_ref.shape[1]

    def group(index, carry):
        first = begin + index * GROUP
        for k in range(GROUP):
            at = jnp.minimum(first + k, last)
            tile = tiles_ref[order_ref[at]].astype(jnp.float32)
            tile = jnp.concatenate([tile, jnp.zeros((rows - lags, width), jnp.float32)], axis=0)
            tile = pltpu.roll(tile, shift_ref[at], 0)
            held[k * rows : (k + 1) * rows, :] = tile.astype(jnp.bfloat16)

        def part(piece, inner):
            span = pl.ds(pl.multiple_of(piece * step, step), step)
            product = jnp.dot(held[...], factor_ref[:, span], preferred_element_type=jnp.float32)
            product = product.astype(jnp.bfloat16)
            for k in range(GROUP):

                @pl.when(first + k < end)
                def _():
                    image_ref[first + k, :, span] = product[k * rows : (k + 1) * rows]

            return inner

        lax.fori_loop(0, columns // step, part, 0)
        return carry

    lax.fori_loop(0, (end - begin + GROUP - 1) // GROUP, group, 0)


def images(order, shift, start, tiles, factor, rows):
    count, lags, width = tiles.shape
    cells, columns = factor.shape
    step = chunk_of(columns, 1024)
    return pl.pallas_call(
        functools.partial(image_kernel, lags, rows, step),
        grid_spec=pltpu.PrefetchScalarGridSpec(
            num_scalar_prefetch=3,
            grid=(cells // width,),
            in_specs=[
                pl.BlockSpec((count, lags, width), lambda i, *_: (0, 0, 0)),
                pl.BlockSpec((width, columns), lambda i, *_: (i, 0)),
            ],
            out_specs=pl.BlockSpec((count, rows, columns), lambda i, *_: (0, 0, 0)),
            scratch_shapes=[pltpu.VMEM((GROUP * rows, width), jnp.bfloat16)],
        ),
        out_shape=jax.ShapeDtypeStruct((count, rows, columns), jnp.bfloat16),
        compiler_params=pltpu.CompilerParams(vmem_limit_bytes=58 * 1024 * 1024),
        cost_estimate=pl.CostEstimate(
            flops=2 * count * rows * width * columns, bytes_accessed=2 * cells * columns, transcendentals=0
        ),
        name="images",
    )(order, shift, start, tiles, factor)


def window_kernel(rows, base_ref, live_ref, factor_ref, state_ref, image_ref, sums_ref, field):
    @pl.when(pl.program_id(0) == 0)
    def _():
        sums_ref[...] = jnp.zeros_like(sums_ref)

    field[...] = jnp.dot(factor_ref[...], state_ref[...], preferred_element_type=jnp.float32)
    columns = state_ref.shape[1]

    def one(at, carry):
        base = pl.multiple_of(base_ref[at], ALIGN)
        product = field[pl.ds(base, rows), :] * image_ref[at].astype(jnp.float32)
        product = jnp.sum(product.reshape(rows // 8, 8, columns), axis=0)
        total = product[:, :128]
        for k in range(1, columns // 128):
            total = total + product[:, k * 128 : (k + 1) * 128]
        sums_ref[at] += total
        return carry

    lax.fori_loop(0, live_ref[0], one, 0)


def window_sums(base, live, factor, state, image):
    hours, columns = state.shape
    count, rows, _ = image.shape
    step = chunk_of(columns, 512)
    return pl.pallas_call(
        functools.partial(window_kernel, rows),
        grid_spec=pltpu.PrefetchScalarGridSpec(
            num_scalar_prefetch=2,
            grid=(columns // step,),
            in_specs=[
                pl.BlockSpec((hours, hours), lambda i, *_: (0, 0)),
                pl.BlockSpec((hours, step), lambda i, *_: (0, i)),
                pl.BlockSpec((count, rows, step), lambda i, *_: (0, 0, i)),
            ],
            out_specs=pl.BlockSpec((count, 8, 128), lambda i, *_: (0, 0, 0)),
            scratch_shapes=[pltpu.VMEM((hours, step), jnp.float32)],
        ),
        out_shape=jax.ShapeDtypeStruct((count, 8, 128), jnp.float32),
        compiler_params=pltpu.CompilerParams(vmem_limit_bytes=58 * 1024 * 1024),
        name="window_sums",
    )(base, live, factor, state, image)


def place_kernel(rows, base_ref, live_ref, weight_ref, image_ref, out_ref, grid):
    grid[...] = jnp.zeros_like(grid)

    def one(at, carry):
        window = pl.ds(pl.multiple_of(base_ref[at], ALIGN), rows)
        grid[window, :] += weight_ref[at] * image_ref[at].astype(jnp.float32)
        return carry

    lax.fori_loop(0, live_ref[0], one, 0)
    out_ref[...] = grid[...].astype(jnp.bfloat16)


def placed(base, live, weight, image, hours):
    count, rows, columns = image.shape
    step = chunk_of(columns, 512)
    return pl.pallas_call(
        functools.partial(place_kernel, rows),
        grid_spec=pltpu.PrefetchScalarGridSpec(
            num_scalar_prefetch=3,
            grid=(columns // step,),
            in_specs=[pl.BlockSpec((count, rows, step), lambda i, *_: (0, 0, i))],
            out_specs=pl.BlockSpec((hours, step), lambda i, *_: (0, i)),
            scratch_shapes=[pltpu.VMEM((hours, step), jnp.float32)],
        ),
        out_shape=jax.ShapeDtypeStruct((hours, columns), jnp.bfloat16),
        compiler_params=pltpu.CompilerParams(vmem_limit_bytes=58 * 1024 * 1024),
        name="placed",
    )(base, live, weight, image)


def gather_kernel(
    n,
    m,
    tiles_ref,
    factor_ref,
    table_ref,
    tiles_out,
    factor_out,
    table_out,
    own_sem,
    table_send,
    table_recv,
    tile_send,
    tile_recv,
    part_send,
    part_recv,
    core_send,
    core_recv,
):
    me, core = lax.axis_index("space"), lax.axis_index("obs")
    slots, block = tiles_ref.shape[0], factor_ref.shape[0]
    part = block // m
    barrier = pltpu.get_barrier_semaphore()
    ways = (1, -1)

    def inside(index):
        return (index >= 0) & (index < n)

    for way in ways:

        @pl.when(inside(me + way))
        def _():
            pl.semaphore_signal(barrier, inc=1, device_id={"space": me + way}, device_id_type=MESH)

    for other in range(1, m):
        pl.semaphore_signal(barrier, inc=1, device_id={"obs": lax.rem(core + other, m)}, device_id_type=MESH)
    ends = jnp.where(me > 0, 1, 0) + jnp.where(me < n - 1, 1, 0)
    pl.semaphore_wait(barrier, ends + (m - 1))

    def tile_rows(index):
        return tiles_out.at[pl.ds(index * slots, slots)]

    def part_rows(index, which):
        start = pl.multiple_of(index * block + which * part, part)
        return factor_out.at[pl.ds(start, part)]

    own_tiles = pltpu.make_async_copy(tiles_ref, tile_rows(me), own_sem.at[0])
    own_factor = pltpu.make_async_copy(
        factor_ref, factor_out.at[pl.ds(pl.multiple_of(me * block, block), block)], own_sem.at[1]
    )
    own_table = pltpu.make_async_copy(table_ref, table_out.at[me], own_sem.at[2])
    own_table.start()
    own_tiles.start()
    own_factor.start()

    def table_copy(d, k, index, first):
        return pltpu.make_async_remote_copy(
            src_ref=table_ref if first else table_out.at[index],
            dst_ref=table_out.at[index],
            send_sem=table_send.at[d, k],
            recv_sem=table_recv.at[d, k],
            device_id={"space": me + ways[d]},
            device_id_type=MESH,
        )

    def tile_copy(d, k, index, first):
        return pltpu.make_async_remote_copy(
            src_ref=tiles_ref if first else tile_rows(index),
            dst_ref=tile_rows(index),
            send_sem=tile_send.at[d, k],
            recv_sem=tile_recv.at[d, k],
            device_id={"space": me + ways[d]},
            device_id_type=MESH,
        )

    def part_copy(d, k, index, first):
        source = factor_ref.at[pl.ds(pl.multiple_of(core * part, part), part)] if first else part_rows(index, core)
        return pltpu.make_async_remote_copy(
            src_ref=source,
            dst_ref=part_rows(index, core),
            send_sem=part_send.at[d, k],
            recv_sem=part_recv.at[d, k],
            device_id={"space": me + ways[d]},
            device_id_type=MESH,
        )

    def core_copy(d, k, other, index, which):
        return pltpu.make_async_remote_copy(
            src_ref=part_rows(index, which),
            dst_ref=part_rows(index, which),
            send_sem=core_send.at[other - 1, d, k],
            recv_sem=core_recv.at[other - 1, d, k],
            device_id={"obs": lax.rem(core + other, m)},
            device_id_type=MESH,
        )

    for k in range(n):
        for d, way in enumerate(ways):
            if k > 0:

                @pl.when(inside(me - way * k))
                def _():
                    table_copy(d, k - 1, me - way * k, False).wait_recv()
                    tile_copy(d, k - 1, me - way * k, False).wait_recv()

            if k < n - 1:

                @pl.when(inside(me - way * k) & inside(me + way))
                def _():
                    table_copy(d, k, me - way * k, k == 0).start()
                    tile_copy(d, k, me - way * k, k == 0).start()

        for d, way in enumerate(ways):
            if k > 0:

                @pl.when(inside(me - way * k))
                def _():
                    part_copy(d, k - 1, me - way * k, False).wait_recv()

            if k < n - 1:

                @pl.when(inside(me - way * k) & inside(me + way))
                def _():
                    part_copy(d, k, me - way * k, k == 0).start()

            if k > 0:

                @pl.when(inside(me - way * k))
                def _():
                    for other in range(1, m):
                        core_copy(d, k - 1, other, me - way * k, core).start()

    for k in range(1, n):
        for d, way in enumerate(ways):

            @pl.when(inside(me - way * k))
            def _():
                for other in range(1, m):
                    came = core_copy(d, k - 1, other, me - way * k, lax.rem(core + m - other, m))
                    came.wait_recv()
                    core_copy(d, k - 1, other, me - way * k, core).wait_send()

    for k in range(n - 1):
        for d, way in enumerate(ways):

            @pl.when(inside(me - way * k) & inside(me + way))
            def _():
                table_copy(d, k, me - way * k, k == 0).wait_send()
                tile_copy(d, k, me - way * k, k == 0).wait_send()
                part_copy(d, k, me - way * k, k == 0).wait_send()

    own_table.wait()
    own_tiles.wait()
    own_factor.wait()


def gathered(footprints, time_factor, table):
    n, m = lax.axis_size("space"), lax.axis_size("obs")
    slots, lags, width = footprints.shape
    block, hours = time_factor.shape
    hops = max(n - 1, 1)
    return pl.pallas_call(
        functools.partial(gather_kernel, n, m),
        out_shape=(
            jax.ShapeDtypeStruct((n * slots, lags, width), footprints.dtype),
            jax.ShapeDtypeStruct((n * block, hours), time_factor.dtype),
            jax.ShapeDtypeStruct((n,) + table.shape, table.dtype),
        ),
        in_specs=[pl.BlockSpec(memory_space=pl.ANY)] * 3,
        out_specs=(pl.BlockSpec(memory_space=pl.ANY),) * 3,
        scratch_shapes=[pltpu.SemaphoreType.DMA((3,))]
        + [pltpu.SemaphoreType.DMA((2, hops))] * 6
        + [pltpu.SemaphoreType.DMA((max(m - 1, 1), 2, hops))] * 2,
        compiler_params=pltpu.CompilerParams(collective_id=0, has_side_effects=True),
        name="gathered",
    )(footprints, time_factor, table)


def total_kernel(axes, sizes, term_ref, out_ref, held, came, send_sem, recv_sem):
    barrier = pltpu.get_barrier_semaphore()
    for axis, size in zip(axes, sizes):
        for other in range(1, size):
            target = lax.rem(lax.axis_index(axis) + other, size)
            pl.semaphore_signal(barrier, inc=1, device_id={axis: target}, device_id_type=MESH)
    pl.semaphore_wait(barrier, sum(sizes) - len(sizes))
    value = term_ref[...]
    at = 0
    for stage, (axis, size) in enumerate(zip(axes, sizes)):
        held[stage] = value
        copies = []
        for other in range(1, size):
            copies.append(
                pltpu.make_async_remote_copy(
                    src_ref=held.at[stage],
                    dst_ref=came.at[at],
                    send_sem=send_sem.at[at],
                    recv_sem=recv_sem.at[at],
                    device_id={axis: lax.rem(lax.axis_index(axis) + other, size)},
                    device_id_type=MESH,
                )
            )
            at += 1
        for copy in copies:
            copy.start()
        for index, copy in enumerate(copies):
            copy.wait()
            value = value + came[at - len(copies) + index]
    out_ref[...] = value


def totals_of(term, axes):
    sizes = [lax.axis_size(axis) for axis in axes]
    copies = max(sum(sizes) - len(sizes), 1)
    length = term.shape[0]
    wide = -(-length // 128) * 128
    padded = jnp.broadcast_to(jnp.pad(term, (0, wide - length))[None, :], (8, wide))
    return pl.pallas_call(
        functools.partial(total_kernel, axes, sizes),
        out_shape=jax.ShapeDtypeStruct((8, wide), jnp.float32),
        in_specs=[pl.BlockSpec(memory_space=pltpu.VMEM)],
        out_specs=pl.BlockSpec(memory_space=pltpu.VMEM),
        scratch_shapes=[
            pltpu.VMEM((len(sizes), 8, wide), jnp.float32),
            pltpu.VMEM((copies, 8, wide), jnp.float32),
            pltpu.SemaphoreType.DMA((copies,)),
            pltpu.SemaphoreType.DMA((copies,)),
        ],
        compiler_params=pltpu.CompilerParams(collective_id=1, has_side_effects=True),
        name="totals",
    )(padded)[0, :length]


def spread_kernel(
    nt, no, step, factor_ref, grid_ref, out_ref, stage, core_in, chip, far_in, core_send, core_recv, far_send, far_recv
):
    tm, core = lax.axis_index("tm"), lax.axis_index("obs")
    hours, columns = grid_ref.shape
    own = hours // (nt * no)
    pieces = columns // step
    barrier = pltpu.get_barrier_semaphore()
    for other in range(1, no):
        pl.semaphore_signal(barrier, inc=1, device_id={"obs": lax.rem(core + other, no)}, device_id_type=MESH)
    for other in range(1, nt):
        pl.semaphore_signal(barrier, inc=1, device_id={"tm": lax.rem(tm + other, nt)}, device_id_type=MESH)
    pl.semaphore_wait(barrier, nt + no - 2)

    def core_copy(piece, other):
        target = lax.rem(core + other, no)
        return pltpu.make_async_remote_copy(
            src_ref=stage.at[piece, target],
            dst_ref=core_in.at[other - 1, piece],
            send_sem=core_send.at[other - 1, piece],
            recv_sem=core_recv.at[other - 1, piece],
            device_id={"obs": target},
            device_id_type=MESH,
        )

    def far_copy(piece, other):
        target = lax.rem(tm + other, nt)
        return pltpu.make_async_remote_copy(
            src_ref=chip.at[piece, target],
            dst_ref=far_in.at[other - 1, piece],
            send_sem=far_send.at[other - 1, piece],
            recv_sem=far_recv.at[other - 1, piece],
            device_id={"tm": target},
            device_id_type=MESH,
        )

    def pair(piece):
        total = stage[piece, core].astype(jnp.float32)
        for other in range(1, no):
            core_copy(piece, other).wait_recv()
            total = total + core_in[other - 1, piece].astype(jnp.float32)
        chip[piece] = total.astype(jnp.bfloat16).reshape(nt, own, step)
        for other in range(1, nt):
            far_copy(piece, other).start()

    def work(piece, carry):
        span = pl.ds(pl.multiple_of(piece * step, step), step)
        product = jnp.dot(factor_ref[...], grid_ref[:, span], preferred_element_type=jnp.float32)
        product = product.astype(jnp.bfloat16)
        for j in range(nt):
            for k in range(no):
                begin = (j * no + k) * own
                stage[piece, k, j * own : (j + 1) * own, :] = product[begin : begin + own]
        for other in range(1, no):
            core_copy(piece, other).start()

        @pl.when(piece > 0)
        def _():
            pair(piece - 1)

        return carry

    lax.fori_loop(0, pieces, work, 0)
    pair(pieces - 1)

    def last(piece, carry):
        span = pl.ds(pl.multiple_of(piece * step, step), step)
        total = chip[piece, tm].astype(jnp.float32)
        for other in range(1, nt):
            far_copy(piece, other).wait_recv()
            total = total + far_in[other - 1, piece].astype(jnp.float32)
        out_ref[:, span] = total.astype(jnp.bfloat16)
        for other in range(1, no):
            core_copy(piece, other).wait_send()
        for other in range(1, nt):
            far_copy(piece, other).wait_send()
        return carry

    lax.fori_loop(0, pieces, last, 0)


def spread_of(factor, grid):
    nt, no = lax.axis_size("tm"), lax.axis_size("obs")
    hours, columns = grid.shape
    own = hours // (nt * no)
    step = chunk_of(columns, 256)
    pieces = columns // step
    far, near = max(nt - 1, 1), max(no - 1, 1)
    return pl.pallas_call(
        functools.partial(spread_kernel, nt, no, step),
        out_shape=jax.ShapeDtypeStruct((own, columns), jnp.bfloat16),
        in_specs=[pl.BlockSpec(memory_space=pltpu.VMEM)] * 2,
        out_specs=pl.BlockSpec(memory_space=pltpu.VMEM),
        scratch_shapes=[
            pltpu.VMEM((pieces, no, nt * own, step), jnp.bfloat16),
            pltpu.VMEM((near, pieces, nt * own, step), jnp.bfloat16),
            pltpu.VMEM((pieces, nt, own, step), jnp.bfloat16),
            pltpu.VMEM((far, pieces, own, step), jnp.bfloat16),
            pltpu.SemaphoreType.DMA((near, pieces)),
            pltpu.SemaphoreType.DMA((near, pieces)),
            pltpu.SemaphoreType.DMA((far, pieces)),
            pltpu.SemaphoreType.DMA((far, pieces)),
        ],
        compiler_params=pltpu.CompilerParams(
            collective_id=2, has_side_effects=True, vmem_limit_bytes=58 * 1024 * 1024
        ),
        name="spread",
    )(factor, grid)


def per_device(
    state,
    spatial_factor,
    time_factor,
    footprints,
    tile_obs,
    tile_block,
    tile_hour,
    tile_count,
    obs_weight,
):
    slots, lags, width = footprints.shape
    blocks = spatial_factor.shape[0] // width
    observations = obs_weight.shape[0]
    rows = -(-lags // ALIGN) * ALIGN + ALIGN
    own_live = (jnp.arange(slots, dtype=jnp.int32)[:, None] < tile_count).astype(jnp.int32)
    table = jnp.concatenate([tile_obs, tile_block, tile_hour, own_live], axis=1)
    table = jnp.pad(table, ((0, 0), (0, 128 - table.shape[1])))
    tiles, factor, table = gathered(footprints, time_factor, table)
    table = table.reshape(-1, 128)[:, :4]
    full_state = lax.all_gather(state, ("tm", "obs"), axis=0, tiled=True)
    hours = factor.shape[0]
    count = tiles.shape[0]

    key = jnp.where(table[:, 3] > 0, table[:, 1], blocks)
    number = jnp.arange(count, dtype=jnp.int32)
    before = (key[None, :] < key[:, None]) | ((key[None, :] == key[:, None]) & (number[None, :] < number[:, None]))
    rank = jnp.sum(before.astype(jnp.int32), axis=1)
    at_rank = (rank[None, :] == number[:, None]).astype(jnp.int32)
    order = jnp.sum(at_rank * number[None, :], axis=1)
    hour = jnp.sum(at_rank * table[:, 2][None, :], axis=1)
    obs = jnp.sum(at_rank * table[:, 0][None, :], axis=1)
    edges = jnp.arange(blocks + 1, dtype=jnp.int32)
    start = jnp.sum((key[None, :] < edges[:, None]).astype(jnp.int32), axis=1)
    live = start[blocks:]
    base = jnp.minimum(hour // ALIGN * ALIGN, hours - rows)
    shift = hour - base

    image = images(order, shift, start, tiles, spatial_factor, rows)
    sums = window_sums(base, live, factor, full_state, image)
    modeled = jnp.where(number < live, jnp.sum(sums, axis=(1, 2)), 0.0)
    onehot = obs[:, None] == jnp.arange(observations, dtype=jnp.int32)[None, :]
    local_totals = jnp.sum(jnp.where(onehot, modeled[:, None], 0.0), axis=0)
    innovation = obs_weight * totals_of(local_totals, ("space", "tm", "obs"))
    weight = jnp.sum(jnp.where(onehot, innovation[None, :], 0.0), axis=1)
    spread = spread_of(factor, placed(base, live, weight, image, hours))
    return state.astype(jnp.float32) + spread.astype(jnp.float32)


def solution(mesh):
    return jax.shard_map(
        per_device,
        mesh=mesh,
        in_specs=(
            P(("groups", "tm", "obs"), "space"),
            P(("tm", "obs"), "space"),
            P("space", None),
            P(("groups", "space"), None, ("tm", "obs")),
            P(("groups", "space"), ("tm", "obs")),
            P(("groups", "space"), ("tm", "obs")),
            P(("groups", "space"), ("tm", "obs")),
            P(("groups", "space"), ("tm", "obs")),
            P("groups"),
        ),
        out_specs=P(("groups", "tm", "obs"), "space"),
        check_vma=False,
    )
```

```python
import functools

import jax
import jax.numpy as jnp
from jax import lax
from jax.experimental import pallas as pl
from jax.experimental.pallas import tpu as pltpu
from jax.sharding import PartitionSpec as P

ALIGN = 16
GROUP = 4
MESH = pl.DeviceIdType.MESH


def chunk_of(columns, most):
    chunk = min(columns, most)
    while columns % chunk:
        chunk //= 2
    return chunk


def image_kernel(
    lags, rows, step, order_ref, shift_ref, start_ref, tiles_ref, factor_ref, image_ref, held, made, busy, made_sem
):
    block = pl.program_id(0)
    begin, end = start_ref[block], start_ref[block + 1]
    last = order_ref.shape[0] - 1
    width = tiles_ref.shape[2]
    columns = factor_ref.shape[1]

    def out_copy(slot, k, at):
        return pltpu.make_async_copy(made.at[slot, k], image_ref.at[at], made_sem.at[slot, k])

    def settle(slot):
        for k in range(GROUP):

            @pl.when(busy[slot * GROUP + k] == 1)
            def _():
                out_copy(slot, k, 0).wait()
                busy[slot * GROUP + k] = 0

    @pl.when(block == 0)
    def _():
        for k in range(2 * GROUP):
            busy[k] = 0
        busy[2 * GROUP] = 0

    def group(index, carry):
        first = begin + index * GROUP
        slot = busy[2 * GROUP]
        busy[2 * GROUP] = 1 - slot
        settle(slot)
        for k in range(GROUP):
            at = jnp.minimum(first + k, last)
            tile = tiles_ref[order_ref[at]].astype(jnp.float32)
            tile = jnp.concatenate([tile, jnp.zeros((rows - lags, width), jnp.float32)], axis=0)
            tile = pltpu.roll(tile, shift_ref[at], 0)
            held[k * rows : (k + 1) * rows, :] = tile.astype(jnp.bfloat16)

        def part(piece, inner):
            span = pl.ds(pl.multiple_of(piece * step, step), step)
            product = jnp.dot(held[...], factor_ref[:, span], preferred_element_type=jnp.float32)
            made[slot, :, :, span] = product.astype(jnp.bfloat16).reshape(GROUP, rows, step)
            return inner

        lax.fori_loop(0, columns // step, part, 0)
        for k in range(GROUP):

            @pl.when(first + k < end)
            def _():
                out_copy(slot, k, first + k).start()
                busy[slot * GROUP + k] = 1

        return carry

    lax.fori_loop(0, (end - begin + GROUP - 1) // GROUP, group, 0)

    @pl.when(block == pl.num_programs(0) - 1)
    def _():
        settle(0)
        settle(1)


def images(order, shift, start, tiles, factor, rows):
    count, lags, width = tiles.shape
    cells, columns = factor.shape
    step = chunk_of(columns, 1024)
    return pl.pallas_call(
        functools.partial(image_kernel, lags, rows, step),
        grid_spec=pltpu.PrefetchScalarGridSpec(
            num_scalar_prefetch=3,
            grid=(cells // width,),
            in_specs=[
                pl.BlockSpec((count, lags, width), lambda i, *_: (0, 0, 0)),
                pl.BlockSpec((width, columns), lambda i, *_: (i, 0)),
            ],
            out_specs=pl.BlockSpec(memory_space=pl.ANY),
            scratch_shapes=[
                pltpu.VMEM((GROUP * rows, width), jnp.bfloat16),
                pltpu.VMEM((2, GROUP, rows, columns), jnp.bfloat16),
                pltpu.SMEM((2 * GROUP + 1,), jnp.int32),
                pltpu.SemaphoreType.DMA((2, GROUP)),
            ],
        ),
        out_shape=jax.ShapeDtypeStruct((count, rows, columns), jnp.bfloat16),
        compiler_params=pltpu.CompilerParams(vmem_limit_bytes=58 * 1024 * 1024),
        cost_estimate=pl.CostEstimate(
            flops=2 * count * rows * width * columns, bytes_accessed=2 * cells * columns, transcendentals=0
        ),
        name="images",
    )(order, shift, start, tiles, factor)


def window_kernel(rows, base_ref, live_ref, factor_ref, state_ref, image_ref, sums_ref, field):
    @pl.when(pl.program_id(0) == 0)
    def _():
        sums_ref[...] = jnp.zeros_like(sums_ref)

    field[...] = jnp.dot(factor_ref[...], state_ref[...], preferred_element_type=jnp.float32)
    columns = state_ref.shape[1]

    def one(at, carry):
        base = pl.multiple_of(base_ref[at], ALIGN)
        product = field[pl.ds(base, rows), :] * image_ref[at].astype(jnp.float32)
        product = jnp.sum(product.reshape(rows // 8, 8, columns), axis=0)
        total = product[:, :128]
        for k in range(1, columns // 128):
            total = total + product[:, k * 128 : (k + 1) * 128]
        sums_ref[at] += total
        return carry

    lax.fori_loop(0, live_ref[0], one, 0)


def window_sums(base, live, factor, state, image):
    hours, columns = state.shape
    count, rows, _ = image.shape
    step = chunk_of(columns, 512)
    return pl.pallas_call(
        functools.partial(window_kernel, rows),
        grid_spec=pltpu.PrefetchScalarGridSpec(
            num_scalar_prefetch=2,
            grid=(columns // step,),
            in_specs=[
                pl.BlockSpec((hours, hours), lambda i, *_: (0, 0)),
                pl.BlockSpec((hours, step), lambda i, *_: (0, i)),
                pl.BlockSpec((count, rows, step), lambda i, *_: (0, 0, i)),
            ],
            out_specs=pl.BlockSpec((count, 8, 128), lambda i, *_: (0, 0, 0)),
            scratch_shapes=[pltpu.VMEM((hours, step), jnp.float32)],
        ),
        out_shape=jax.ShapeDtypeStruct((count, 8, 128), jnp.float32),
        compiler_params=pltpu.CompilerParams(vmem_limit_bytes=58 * 1024 * 1024),
        name="window_sums",
    )(base, live, factor, state, image)


def place_kernel(rows, base_ref, live_ref, weight_ref, image_ref, out_ref, grid):
    grid[...] = jnp.zeros_like(grid)

    def one(at, carry):
        window = pl.ds(pl.multiple_of(base_ref[at], ALIGN), rows)
        grid[window, :] += weight_ref[at] * image_ref[at].astype(jnp.float32)
        return carry

    lax.fori_loop(0, live_ref[0], one, 0)
    out_ref[...] = grid[...].astype(jnp.bfloat16)


def placed(base, live, weight, image, hours):
    count, rows, columns = image.shape
    step = chunk_of(columns, 512)
    return pl.pallas_call(
        functools.partial(place_kernel, rows),
        grid_spec=pltpu.PrefetchScalarGridSpec(
            num_scalar_prefetch=3,
            grid=(columns // step,),
            in_specs=[pl.BlockSpec((count, rows, step), lambda i, *_: (0, 0, i))],
            out_specs=pl.BlockSpec((hours, step), lambda i, *_: (0, i)),
            scratch_shapes=[pltpu.VMEM((hours, step), jnp.float32)],
        ),
        out_shape=jax.ShapeDtypeStruct((hours, columns), jnp.bfloat16),
        compiler_params=pltpu.CompilerParams(vmem_limit_bytes=58 * 1024 * 1024),
        name="placed",
    )(base, live, weight, image)


def gather_kernel(
    n,
    m,
    g,
    tiles_ref,
    factor_ref,
    table_ref,
    tiles_out,
    factor_out,
    table_out,
    own_sem,
    table_send,
    table_recv,
    tile_send,
    tile_recv,
    part_send,
    part_recv,
    core_send,
    core_recv,
):
    me, obs, side = lax.axis_index("space"), lax.axis_index("obs"), lax.axis_index("groups")
    core = side * m + obs
    slots, block = tiles_ref.shape[0], factor_ref.shape[0]
    part = block // (m * g)
    others = [(i, j) for i in range(g) for j in range(m) if i or j]
    barrier = pltpu.get_barrier_semaphore()
    ways = (1, -1)

    def inside(index):
        return (index >= 0) & (index < n)

    for way in ways:

        @pl.when(inside(me + way))
        def _():
            pl.semaphore_signal(barrier, inc=1, device_id={"space": me + way}, device_id_type=MESH)

    for i, j in others:
        pl.semaphore_signal(
            barrier,
            inc=1,
            device_id={"groups": lax.rem(side + i, g), "obs": lax.rem(obs + j, m)},
            device_id_type=MESH,
        )
    ends = jnp.where(me > 0, 1, 0) + jnp.where(me < n - 1, 1, 0)
    pl.semaphore_wait(barrier, ends + len(others))

    def tile_rows(index):
        return tiles_out.at[pl.ds(index * slots, slots)]

    def part_rows(index, which):
        start = pl.multiple_of(index * block + which * part, part)
        return factor_out.at[pl.ds(start, part)]

    own_tiles = pltpu.make_async_copy(tiles_ref, tile_rows(me), own_sem.at[0])
    own_factor = pltpu.make_async_copy(
        factor_ref, factor_out.at[pl.ds(pl.multiple_of(me * block, block), block)], own_sem.at[1]
    )
    own_table = pltpu.make_async_copy(table_ref, table_out.at[me], own_sem.at[2])
    own_table.start()
    own_tiles.start()
    own_factor.start()

    def table_copy(d, k, index, first):
        return pltpu.make_async_remote_copy(
            src_ref=table_ref if first else table_out.at[index],
            dst_ref=table_out.at[index],
            send_sem=table_send.at[d, k],
            recv_sem=table_recv.at[d, k],
            device_id={"space": me + ways[d]},
            device_id_type=MESH,
        )

    def tile_copy(d, k, index, first):
        return pltpu.make_async_remote_copy(
            src_ref=tiles_ref if first else tile_rows(index),
            dst_ref=tile_rows(index),
            send_sem=tile_send.at[d, k],
            recv_sem=tile_recv.at[d, k],
            device_id={"space": me + ways[d]},
            device_id_type=MESH,
        )

    def part_copy(d, k, index, first):
        source = factor_ref.at[pl.ds(pl.multiple_of(core * part, part), part)] if first else part_rows(index, core)
        return pltpu.make_async_remote_copy(
            src_ref=source,
            dst_ref=part_rows(index, core),
            send_sem=part_send.at[d, k],
            recv_sem=part_recv.at[d, k],
            device_id={"space": me + ways[d]},
            device_id_type=MESH,
        )

    def core_copy(d, k, other, index, which):
        return pltpu.make_async_remote_copy(
            src_ref=part_rows(index, which),
            dst_ref=part_rows(index, which),
            send_sem=core_send.at[other, d, k],
            recv_sem=core_recv.at[other, d, k],
            device_id={"groups": lax.rem(side + others[other][0], g), "obs": lax.rem(obs + others[other][1], m)},
            device_id_type=MESH,
        )

    for k in range(n):
        for d, way in enumerate(ways):
            if k > 0:

                @pl.when(inside(me - way * k))
                def _():
                    table_copy(d, k - 1, me - way * k, False).wait_recv()
                    tile_copy(d, k - 1, me - way * k, False).wait_recv()

            if k < n - 1:

                @pl.when(inside(me - way * k) & inside(me + way))
                def _():
                    table_copy(d, k, me - way * k, k == 0).start()
                    tile_copy(d, k, me - way * k, k == 0).start()

        for d, way in enumerate(ways):
            if k > 0:

                @pl.when(inside(me - way * k))
                def _():
                    part_copy(d, k - 1, me - way * k, False).wait_recv()

            if k < n - 1:

                @pl.when(inside(me - way * k) & inside(me + way))
                def _():
                    part_copy(d, k, me - way * k, k == 0).start()

            if k > 0:

                @pl.when(inside(me - way * k))
                def _():
                    for other in range(len(others)):
                        core_copy(d, k - 1, other, me - way * k, core).start()

    for k in range(1, n):
        for d, way in enumerate(ways):

            @pl.when(inside(me - way * k))
            def _():
                for other, (i, j) in enumerate(others):
                    source = lax.rem(side + g - i, g) * m + lax.rem(obs + m - j, m)
                    came = core_copy(d, k - 1, other, me - way * k, source)
                    came.wait_recv()
                    core_copy(d, k - 1, other, me - way * k, core).wait_send()

    for k in range(n - 1):
        for d, way in enumerate(ways):

            @pl.when(inside(me - way * k) & inside(me + way))
            def _():
                table_copy(d, k, me - way * k, k == 0).wait_send()
                tile_copy(d, k, me - way * k, k == 0).wait_send()
                part_copy(d, k, me - way * k, k == 0).wait_send()

    own_table.wait()
    own_tiles.wait()
    own_factor.wait()


def gathered(footprints, time_factor, table):
    n, m, g = lax.axis_size("space"), lax.axis_size("obs"), lax.axis_size("groups")
    slots, lags, width = footprints.shape
    block, hours = time_factor.shape
    hops = max(n - 1, 1)
    return pl.pallas_call(
        functools.partial(gather_kernel, n, m, g),
        out_shape=(
            jax.ShapeDtypeStruct((n * slots, lags, width), footprints.dtype),
            jax.ShapeDtypeStruct((n * block, hours), time_factor.dtype),
            jax.ShapeDtypeStruct((n,) + table.shape, table.dtype),
        ),
        in_specs=[pl.BlockSpec(memory_space=pl.ANY)] * 3,
        out_specs=(pl.BlockSpec(memory_space=pl.ANY),) * 3,
        scratch_shapes=[pltpu.SemaphoreType.DMA((3,))]
        + [pltpu.SemaphoreType.DMA((2, hops))] * 6
        + [pltpu.SemaphoreType.DMA((max(m * g - 1, 1), 2, hops))] * 2,
        compiler_params=pltpu.CompilerParams(collective_id=0, has_side_effects=True),
        name="gathered",
    )(footprints, time_factor, table)


def total_kernel(axes, sizes, sums_ref, obs_ref, gain_ref, out_ref, held, came, send_sem, recv_sem):
    barrier = pltpu.get_barrier_semaphore()
    for axis, size in zip(axes, sizes):
        for other in range(1, size):
            target = lax.rem(lax.axis_index(axis) + other, size)
            pl.semaphore_signal(barrier, inc=1, device_id={axis: target}, device_id_type=MESH)
    pl.semaphore_wait(barrier, sum(sizes) - len(sizes))
    count, wide = out_ref.shape[0], gain_ref.shape[1]
    modeled = jnp.sum(jnp.sum(sums_ref[...], axis=1), axis=1, keepdims=True)
    onehot = obs_ref[:, :1] == lax.broadcasted_iota(jnp.int32, (count, wide), 1)
    value = jnp.sum(jnp.where(onehot, modeled, 0.0), axis=0, keepdims=True)
    value = jnp.broadcast_to(value, (8, wide))
    at = 0
    for stage, (axis, size) in enumerate(zip(axes, sizes)):
        held[stage] = value
        copies = []
        for other in range(1, size):
            copies.append(
                pltpu.make_async_remote_copy(
                    src_ref=held.at[stage],
                    dst_ref=came.at[at],
                    send_sem=send_sem.at[at],
                    recv_sem=recv_sem.at[at],
                    device_id={axis: lax.rem(lax.axis_index(axis) + other, size)},
                    device_id_type=MESH,
                )
            )
            at += 1
        for copy in copies:
            copy.start()
        for index, copy in enumerate(copies):
            copy.wait()
            value = value + came[at - len(copies) + index]
    innovation = gain_ref[:1] * value[:1]
    weight = jnp.sum(jnp.where(onehot, innovation, 0.0), axis=1, keepdims=True)
    out_ref[...] = jnp.broadcast_to(weight, out_ref.shape)


def weights_of(sums, obs, gain, axes):
    sizes = [lax.axis_size(axis) for axis in axes]
    copies = max(sum(sizes) - len(sizes), 1)
    length, count = gain.shape[0], obs.shape[0]
    wide = -(-length // 128) * 128
    gain = jnp.broadcast_to(jnp.pad(gain, (0, wide - length))[None, :], (8, wide))
    obs = jnp.broadcast_to(obs[:, None], (count, 128))
    return pl.pallas_call(
        functools.partial(total_kernel, axes, sizes),
        out_shape=jax.ShapeDtypeStruct((count, 128), jnp.float32),
        in_specs=[pl.BlockSpec(memory_space=pltpu.VMEM)] * 3,
        out_specs=pl.BlockSpec(memory_space=pltpu.VMEM),
        scratch_shapes=[
            pltpu.VMEM((len(sizes), 8, wide), jnp.float32),
            pltpu.VMEM((copies, 8, wide), jnp.float32),
            pltpu.SemaphoreType.DMA((copies,)),
            pltpu.SemaphoreType.DMA((copies,)),
        ],
        compiler_params=pltpu.CompilerParams(collective_id=1, has_side_effects=True),
        name="totals",
    )(sums, obs, gain)[:, 0]


def spread_kernel(
    nt,
    no,
    step,
    factor_ref,
    grid_ref,
    out_ref,
    stage,
    core_in,
    chip,
    far_in,
    near_grid,
    grid_sem,
    core_send,
    core_recv,
    far_send,
    far_recv,
):
    tm, core = lax.axis_index("tm"), lax.axis_index("obs")
    hours, columns = grid_ref.shape
    own = hours // (nt * no)
    pieces = columns // step

    def fetch(piece):
        span = pl.ds(pl.multiple_of(piece * step, step), step)
        return pltpu.make_async_copy(grid_ref.at[:, span], near_grid.at[piece], grid_sem.at[piece])

    def begin(piece, carry):
        fetch(piece).start()
        return carry

    lax.fori_loop(0, pieces, begin, 0)
    barrier = pltpu.get_barrier_semaphore()
    for other in range(1, no):
        pl.semaphore_signal(barrier, inc=1, device_id={"obs": lax.rem(core + other, no)}, device_id_type=MESH)
    for other in range(1, nt):
        pl.semaphore_signal(barrier, inc=1, device_id={"tm": lax.rem(tm + other, nt)}, device_id_type=MESH)
    pl.semaphore_wait(barrier, nt + no - 2)

    def core_copy(piece, other):
        target = lax.rem(core + other, no)
        return pltpu.make_async_remote_copy(
            src_ref=stage.at[piece, target],
            dst_ref=core_in.at[other - 1, piece],
            send_sem=core_send.at[other - 1, piece],
            recv_sem=core_recv.at[other - 1, piece],
            device_id={"obs": target},
            device_id_type=MESH,
        )

    def far_copy(piece, other):
        target = lax.rem(tm + other, nt)
        return pltpu.make_async_remote_copy(
            src_ref=chip.at[piece, target],
            dst_ref=far_in.at[other - 1, piece],
            send_sem=far_send.at[other - 1, piece],
            recv_sem=far_recv.at[other - 1, piece],
            device_id={"tm": target},
            device_id_type=MESH,
        )

    def pair(piece):
        total = stage[piece, core].astype(jnp.float32)
        for other in range(1, no):
            core_copy(piece, other).wait_recv()
            total = total + core_in[other - 1, piece].astype(jnp.float32)
        chip[piece] = total.astype(jnp.bfloat16).reshape(nt, own, step)
        for other in range(1, nt):
            far_copy(piece, other).start()

    def work(piece, carry):
        fetch(piece).wait()
        product = jnp.dot(factor_ref[...], near_grid[piece], preferred_element_type=jnp.float32)
        product = product.astype(jnp.bfloat16)
        for j in range(nt):
            for k in range(no):
                row = (j * no + k) * own
                stage[piece, k, j * own : (j + 1) * own, :] = product[row : row + own]
        for other in range(1, no):
            core_copy(piece, other).start()

        @pl.when(piece > 0)
        def _():
            pair(piece - 1)

        return carry

    lax.fori_loop(0, pieces, work, 0)
    pair(pieces - 1)

    def last(piece, carry):
        span = pl.ds(pl.multiple_of(piece * step, step), step)
        total = chip[piece, tm].astype(jnp.float32)
        for other in range(1, nt):
            far_copy(piece, other).wait_recv()
            total = total + far_in[other - 1, piece].astype(jnp.float32)
        out_ref[:, span] = total.astype(jnp.bfloat16)
        for other in range(1, no):
            core_copy(piece, other).wait_send()
        for other in range(1, nt):
            far_copy(piece, other).wait_send()
        return carry

    lax.fori_loop(0, pieces, last, 0)


def spread_of(factor, grid):
    nt, no = lax.axis_size("tm"), lax.axis_size("obs")
    hours, columns = grid.shape
    own = hours // (nt * no)
    step = chunk_of(columns, 256)
    pieces = columns // step
    far, near = max(nt - 1, 1), max(no - 1, 1)
    return pl.pallas_call(
        functools.partial(spread_kernel, nt, no, step),
        out_shape=jax.ShapeDtypeStruct((own, columns), jnp.bfloat16),
        in_specs=[pl.BlockSpec(memory_space=pltpu.VMEM), pl.BlockSpec(memory_space=pl.ANY)],
        out_specs=pl.BlockSpec(memory_space=pltpu.VMEM),
        scratch_shapes=[
            pltpu.VMEM((pieces, no, nt * own, step), jnp.bfloat16),
            pltpu.VMEM((near, pieces, nt * own, step), jnp.bfloat16),
            pltpu.VMEM((pieces, nt, own, step), jnp.bfloat16),
            pltpu.VMEM((far, pieces, own, step), jnp.bfloat16),
            pltpu.VMEM((pieces, hours, step), jnp.bfloat16),
            pltpu.SemaphoreType.DMA((pieces,)),
            pltpu.SemaphoreType.DMA((near, pieces)),
            pltpu.SemaphoreType.DMA((near, pieces)),
            pltpu.SemaphoreType.DMA((far, pieces)),
            pltpu.SemaphoreType.DMA((far, pieces)),
        ],
        compiler_params=pltpu.CompilerParams(
            collective_id=2, has_side_effects=True, vmem_limit_bytes=58 * 1024 * 1024
        ),
        name="spread",
    )(factor, grid)


def per_device(
    state,
    spatial_factor,
    time_factor,
    footprints,
    tile_obs,
    tile_block,
    tile_hour,
    tile_count,
    obs_weight,
):
    slots, lags, width = footprints.shape
    blocks = spatial_factor.shape[0] // width
    rows = -(-lags // ALIGN) * ALIGN + ALIGN
    own_live = (jnp.arange(slots, dtype=jnp.int32)[:, None] < tile_count).astype(jnp.int32)
    table = jnp.concatenate([tile_obs, tile_block, tile_hour, own_live], axis=1)
    table = jnp.pad(table, ((0, 0), (0, 128 - table.shape[1])))
    tiles, factor, table = gathered(footprints, time_factor, table)
    table = table.reshape(-1, 128)[:, :4]
    full_state = lax.all_gather(state, ("tm", "obs"), axis=0, tiled=True)
    hours = factor.shape[0]
    count = tiles.shape[0]

    key = jnp.where(table[:, 3] > 0, table[:, 1], blocks)
    number = jnp.arange(count, dtype=jnp.int32)
    before = (key[None, :] < key[:, None]) | ((key[None, :] == key[:, None]) & (number[None, :] < number[:, None]))
    rank = jnp.sum(before.astype(jnp.int32), axis=1)
    at_rank = (rank[None, :] == number[:, None]).astype(jnp.int32)
    order = jnp.sum(at_rank * number[None, :], axis=1)
    hour = jnp.sum(at_rank * table[:, 2][None, :], axis=1)
    obs = jnp.sum(at_rank * table[:, 0][None, :], axis=1)
    edges = jnp.arange(blocks + 1, dtype=jnp.int32)
    start = jnp.sum((key[None, :] < edges[:, None]).astype(jnp.int32), axis=1)
    live = start[blocks:]
    base = jnp.minimum(hour // ALIGN * ALIGN, hours - rows)
    shift = hour - base

    image = images(order, shift, start, tiles, spatial_factor, rows)
    sums = window_sums(base, live, factor, full_state, image)
    weight = weights_of(sums, obs, obs_weight, ("space", "tm", "obs"))
    spread = spread_of(factor, placed(base, live, weight, image, hours))
    return state.astype(jnp.float32) + spread.astype(jnp.float32)


def solution(mesh):
    return jax.shard_map(
        per_device,
        mesh=mesh,
        in_specs=(
            P(("groups", "tm", "obs"), "space"),
            P(("tm", "obs"), "space"),
            P("space", None),
            P(("groups", "space"), None, ("tm", "obs")),
            P(("groups", "space"), ("tm", "obs")),
            P(("groups", "space"), ("tm", "obs")),
            P(("groups", "space"), ("tm", "obs")),
            P(("groups", "space"), ("tm", "obs")),
            P("groups"),
        ),
        out_specs=P(("groups", "tm", "obs"), "space"),
        check_vma=False,
    )
```

```python
import functools

import jax
import jax.numpy as jnp
from jax import lax
from jax.experimental import pallas as pl
from jax.experimental.pallas import tpu as pltpu
from jax.sharding import PartitionSpec as P

ALIGN = 16
GROUP = 4
MESH = pl.DeviceIdType.MESH


def chunk_of(columns, most):
    chunk = min(columns, most)
    while columns % chunk:
        chunk //= 2
    return chunk


def image_kernel(
    lags, rows, step, order_ref, shift_ref, start_ref, tiles_ref, factor_ref, image_ref, held, made, busy, made_sem
):
    block = pl.program_id(0)
    begin, end = start_ref[block], start_ref[block + 1]
    last = order_ref.shape[0] - 1
    width = tiles_ref.shape[2]
    columns = factor_ref.shape[1]

    def out_copy(slot, k, at):
        return pltpu.make_async_copy(made.at[slot, k], image_ref.at[at], made_sem.at[slot, k])

    def settle(slot):
        for k in range(GROUP):

            @pl.when(busy[slot * GROUP + k] == 1)
            def _():
                out_copy(slot, k, 0).wait()
                busy[slot * GROUP + k] = 0

    @pl.when(block == 0)
    def _():
        for k in range(2 * GROUP):
            busy[k] = 0
        busy[2 * GROUP] = 0

    def group(index, carry):
        first = begin + index * GROUP
        slot = busy[2 * GROUP]
        busy[2 * GROUP] = 1 - slot
        settle(slot)
        for k in range(GROUP):
            at = jnp.minimum(first + k, last)
            tile = tiles_ref[order_ref[at]].astype(jnp.float32)
            tile = jnp.concatenate([tile, jnp.zeros((rows - lags, width), jnp.float32)], axis=0)
            tile = pltpu.roll(tile, shift_ref[at], 0)
            held[k * rows : (k + 1) * rows, :] = tile.astype(jnp.bfloat16)

        def part(piece, inner):
            span = pl.ds(pl.multiple_of(piece * step, step), step)
            product = jnp.dot(held[...], factor_ref[:, span], preferred_element_type=jnp.float32)
            made[slot, :, :, span] = product.astype(jnp.bfloat16).reshape(GROUP, rows, step)
            return inner

        lax.fori_loop(0, columns // step, part, 0)
        for k in range(GROUP):

            @pl.when(first + k < end)
            def _():
                out_copy(slot, k, first + k).start()
                busy[slot * GROUP + k] = 1

        return carry

    lax.fori_loop(0, (end - begin + GROUP - 1) // GROUP, group, 0)

    @pl.when(block == pl.num_programs(0) - 1)
    def _():
        settle(0)
        settle(1)


def images(order, shift, start, tiles, factor, rows):
    count, lags, width = tiles.shape
    cells, columns = factor.shape
    step = chunk_of(columns, 1024)
    return pl.pallas_call(
        functools.partial(image_kernel, lags, rows, step),
        grid_spec=pltpu.PrefetchScalarGridSpec(
            num_scalar_prefetch=3,
            grid=(cells // width,),
            in_specs=[
                pl.BlockSpec((count, lags, width), lambda i, *_: (0, 0, 0)),
                pl.BlockSpec((width, columns), lambda i, *_: (i, 0)),
            ],
            out_specs=pl.BlockSpec(memory_space=pl.ANY),
            scratch_shapes=[
                pltpu.VMEM((GROUP * rows, width), jnp.bfloat16),
                pltpu.VMEM((2, GROUP, rows, columns), jnp.bfloat16),
                pltpu.SMEM((2 * GROUP + 1,), jnp.int32),
                pltpu.SemaphoreType.DMA((2, GROUP)),
            ],
        ),
        out_shape=jax.ShapeDtypeStruct((count, rows, columns), jnp.bfloat16),
        compiler_params=pltpu.CompilerParams(vmem_limit_bytes=58 * 1024 * 1024),
        cost_estimate=pl.CostEstimate(
            flops=2 * count * rows * width * columns, bytes_accessed=2 * cells * columns, transcendentals=0
        ),
        name="images",
    )(order, shift, start, tiles, factor)


def window_kernel(rows, base_ref, live_ref, factor_ref, state_ref, image_ref, sums_ref, field):
    @pl.when(pl.program_id(0) == 0)
    def _():
        sums_ref[...] = jnp.zeros_like(sums_ref)

    field[...] = jnp.dot(factor_ref[...], state_ref[...], preferred_element_type=jnp.float32)
    columns = state_ref.shape[1]

    def one(at, carry):
        base = pl.multiple_of(base_ref[at], ALIGN)
        product = field[pl.ds(base, rows), :] * image_ref[at].astype(jnp.float32)
        product = jnp.sum(product.reshape(rows // 8, 8, columns), axis=0)
        total = product[:, :128]
        for k in range(1, columns // 128):
            total = total + product[:, k * 128 : (k + 1) * 128]
        sums_ref[at] += total
        return carry

    lax.fori_loop(0, live_ref[0], one, 0)


def window_sums(base, live, factor, state, image):
    hours, columns = state.shape
    count, rows, _ = image.shape
    step = chunk_of(columns, 1024)
    return pl.pallas_call(
        functools.partial(window_kernel, rows),
        grid_spec=pltpu.PrefetchScalarGridSpec(
            num_scalar_prefetch=2,
            grid=(columns // step,),
            in_specs=[
                pl.BlockSpec((hours, hours), lambda i, *_: (0, 0)),
                pl.BlockSpec((hours, step), lambda i, *_: (0, i)),
                pl.BlockSpec((count, rows, step), lambda i, *_: (0, 0, i)),
            ],
            out_specs=pl.BlockSpec((count, 8, 128), lambda i, *_: (0, 0, 0)),
            scratch_shapes=[pltpu.VMEM((hours, step), jnp.float32)],
        ),
        out_shape=jax.ShapeDtypeStruct((count, 8, 128), jnp.float32),
        compiler_params=pltpu.CompilerParams(vmem_limit_bytes=58 * 1024 * 1024),
        name="window_sums",
    )(base, live, factor, state, image)


def place_kernel(rows, base_ref, live_ref, weight_ref, image_ref, out_ref, grid):
    grid[...] = jnp.zeros_like(grid)

    def one(at, carry):
        window = pl.ds(pl.multiple_of(base_ref[at], ALIGN), rows)
        grid[window, :] += weight_ref[at] * image_ref[at].astype(jnp.float32)
        return carry

    lax.fori_loop(0, live_ref[0], one, 0)
    out_ref[...] = grid[...].astype(jnp.bfloat16)


def placed(base, live, weight, image, hours):
    count, rows, columns = image.shape
    step = chunk_of(columns, 1024)
    return pl.pallas_call(
        functools.partial(place_kernel, rows),
        grid_spec=pltpu.PrefetchScalarGridSpec(
            num_scalar_prefetch=3,
            grid=(columns // step,),
            in_specs=[pl.BlockSpec((count, rows, step), lambda i, *_: (0, 0, i))],
            out_specs=pl.BlockSpec((hours, step), lambda i, *_: (0, i)),
            scratch_shapes=[pltpu.VMEM((hours, step), jnp.float32)],
        ),
        out_shape=jax.ShapeDtypeStruct((hours, columns), jnp.bfloat16),
        compiler_params=pltpu.CompilerParams(vmem_limit_bytes=58 * 1024 * 1024),
        name="placed",
    )(base, live, weight, image)


def gather_kernel(
    n,
    m,
    g,
    tiles_ref,
    factor_ref,
    table_ref,
    tiles_out,
    factor_out,
    table_out,
    own_sem,
    table_send,
    table_recv,
    tile_send,
    tile_recv,
    part_send,
    part_recv,
    core_send,
    core_recv,
):
    me, obs, side = lax.axis_index("space"), lax.axis_index("obs"), lax.axis_index("groups")
    core = side * m + obs
    slots, block = tiles_ref.shape[0], factor_ref.shape[0]
    part = block // (m * g)
    others = [(i, j) for i in range(g) for j in range(m) if i or j]
    barrier = pltpu.get_barrier_semaphore()
    ways = (1, -1)

    def inside(index):
        return (index >= 0) & (index < n)

    for way in ways:

        @pl.when(inside(me + way))
        def _():
            pl.semaphore_signal(barrier, inc=1, device_id={"space": me + way}, device_id_type=MESH)

    for i, j in others:
        pl.semaphore_signal(
            barrier,
            inc=1,
            device_id={"groups": lax.rem(side + i, g), "obs": lax.rem(obs + j, m)},
            device_id_type=MESH,
        )
    ends = jnp.where(me > 0, 1, 0) + jnp.where(me < n - 1, 1, 0)
    pl.semaphore_wait(barrier, ends + len(others))

    def tile_rows(index):
        return tiles_out.at[pl.ds(index * slots, slots)]

    def part_rows(index, which):
        start = pl.multiple_of(index * block + which * part, part)
        return factor_out.at[pl.ds(start, part)]

    own_tiles = pltpu.make_async_copy(tiles_ref, tile_rows(me), own_sem.at[0])
    own_factor = pltpu.make_async_copy(
        factor_ref, factor_out.at[pl.ds(pl.multiple_of(me * block, block), block)], own_sem.at[1]
    )
    own_table = pltpu.make_async_copy(table_ref, table_out.at[me], own_sem.at[2])
    own_table.start()
    own_tiles.start()
    own_factor.start()

    def table_copy(d, k, index, first):
        return pltpu.make_async_remote_copy(
            src_ref=table_ref if first else table_out.at[index],
            dst_ref=table_out.at[index],
            send_sem=table_send.at[d, k],
            recv_sem=table_recv.at[d, k],
            device_id={"space": me + ways[d]},
            device_id_type=MESH,
        )

    def tile_copy(d, k, index, first):
        return pltpu.make_async_remote_copy(
            src_ref=tiles_ref if first else tile_rows(index),
            dst_ref=tile_rows(index),
            send_sem=tile_send.at[d, k],
            recv_sem=tile_recv.at[d, k],
            device_id={"space": me + ways[d]},
            device_id_type=MESH,
        )

    def part_copy(d, k, index, first):
        source = factor_ref.at[pl.ds(pl.multiple_of(core * part, part), part)] if first else part_rows(index, core)
        return pltpu.make_async_remote_copy(
            src_ref=source,
            dst_ref=part_rows(index, core),
            send_sem=part_send.at[d, k],
            recv_sem=part_recv.at[d, k],
            device_id={"space": me + ways[d]},
            device_id_type=MESH,
        )

    def core_copy(d, k, other, index, which):
        return pltpu.make_async_remote_copy(
            src_ref=part_rows(index, which),
            dst_ref=part_rows(index, which),
            send_sem=core_send.at[other, d, k],
            recv_sem=core_recv.at[other, d, k],
            device_id={"groups": lax.rem(side + others[other][0], g), "obs": lax.rem(obs + others[other][1], m)},
            device_id_type=MESH,
        )

    for k in range(n):
        for d, way in enumerate(ways):
            if k > 0:

                @pl.when(inside(me - way * k))
                def _():
                    table_copy(d, k - 1, me - way * k, False).wait_recv()
                    tile_copy(d, k - 1, me - way * k, False).wait_recv()

            if k < n - 1:

                @pl.when(inside(me - way * k) & inside(me + way))
                def _():
                    table_copy(d, k, me - way * k, k == 0).start()
                    tile_copy(d, k, me - way * k, k == 0).start()

        for d, way in enumerate(ways):
            if k > 0:

                @pl.when(inside(me - way * k))
                def _():
                    part_copy(d, k - 1, me - way * k, False).wait_recv()

            if k < n - 1:

                @pl.when(inside(me - way * k) & inside(me + way))
                def _():
                    part_copy(d, k, me - way * k, k == 0).start()

            if k > 0:

                @pl.when(inside(me - way * k))
                def _():
                    for other in range(len(others)):
                        core_copy(d, k - 1, other, me - way * k, core).start()

    for k in range(1, n):
        for d, way in enumerate(ways):

            @pl.when(inside(me - way * k))
            def _():
                for other, (i, j) in enumerate(others):
                    source = lax.rem(side + g - i, g) * m + lax.rem(obs + m - j, m)
                    came = core_copy(d, k - 1, other, me - way * k, source)
                    came.wait_recv()
                    core_copy(d, k - 1, other, me - way * k, core).wait_send()

    for k in range(n - 1):
        for d, way in enumerate(ways):

            @pl.when(inside(me - way * k) & inside(me + way))
            def _():
                table_copy(d, k, me - way * k, k == 0).wait_send()
                tile_copy(d, k, me - way * k, k == 0).wait_send()
                part_copy(d, k, me - way * k, k == 0).wait_send()

    own_table.wait()
    own_tiles.wait()
    own_factor.wait()


def gathered(footprints, time_factor, table):
    n, m, g = lax.axis_size("space"), lax.axis_size("obs"), lax.axis_size("groups")
    slots, lags, width = footprints.shape
    block, hours = time_factor.shape
    hops = max(n - 1, 1)
    return pl.pallas_call(
        functools.partial(gather_kernel, n, m, g),
        out_shape=(
            jax.ShapeDtypeStruct((n * slots, lags, width), footprints.dtype),
            jax.ShapeDtypeStruct((n * block, hours), time_factor.dtype),
            jax.ShapeDtypeStruct((n,) + table.shape, table.dtype),
        ),
        in_specs=[pl.BlockSpec(memory_space=pl.ANY)] * 3,
        out_specs=(pl.BlockSpec(memory_space=pl.ANY),) * 3,
        scratch_shapes=[pltpu.SemaphoreType.DMA((3,))]
        + [pltpu.SemaphoreType.DMA((2, hops))] * 6
        + [pltpu.SemaphoreType.DMA((max(m * g - 1, 1), 2, hops))] * 2,
        compiler_params=pltpu.CompilerParams(collective_id=0, has_side_effects=True),
        name="gathered",
    )(footprints, time_factor, table)


def total_kernel(axes, sizes, sums_ref, obs_ref, gain_ref, out_ref, held, came, send_sem, recv_sem):
    barrier = pltpu.get_barrier_semaphore()
    for axis, size in zip(axes, sizes):
        for other in range(1, size):
            target = lax.rem(lax.axis_index(axis) + other, size)
            pl.semaphore_signal(barrier, inc=1, device_id={axis: target}, device_id_type=MESH)
    pl.semaphore_wait(barrier, sum(sizes) - len(sizes))
    count, wide = out_ref.shape[0], gain_ref.shape[1]
    modeled = jnp.sum(jnp.sum(sums_ref[...], axis=1), axis=1, keepdims=True)
    onehot = obs_ref[:, :1] == lax.broadcasted_iota(jnp.int32, (count, wide), 1)
    value = jnp.sum(jnp.where(onehot, modeled, 0.0), axis=0, keepdims=True)
    value = jnp.broadcast_to(value, (8, wide))
    at = 0
    for stage, (axis, size) in enumerate(zip(axes, sizes)):
        held[stage] = value
        copies = []
        for other in range(1, size):
            copies.append(
                pltpu.make_async_remote_copy(
                    src_ref=held.at[stage],
                    dst_ref=came.at[at],
                    send_sem=send_sem.at[at],
                    recv_sem=recv_sem.at[at],
                    device_id={axis: lax.rem(lax.axis_index(axis) + other, size)},
                    device_id_type=MESH,
                )
            )
            at += 1
        for copy in copies:
            copy.start()
        for index, copy in enumerate(copies):
            copy.wait()
            value = value + came[at - len(copies) + index]
    innovation = gain_ref[:1] * value[:1]
    weight = jnp.sum(jnp.where(onehot, innovation, 0.0), axis=1, keepdims=True)
    out_ref[...] = jnp.broadcast_to(weight, out_ref.shape)


def weights_of(sums, obs, gain, axes):
    sizes = [lax.axis_size(axis) for axis in axes]
    copies = max(sum(sizes) - len(sizes), 1)
    length, count = gain.shape[0], obs.shape[0]
    wide = -(-length // 128) * 128
    gain = jnp.broadcast_to(jnp.pad(gain, (0, wide - length))[None, :], (8, wide))
    obs = jnp.broadcast_to(obs[:, None], (count, 128))
    return pl.pallas_call(
        functools.partial(total_kernel, axes, sizes),
        out_shape=jax.ShapeDtypeStruct((count, 128), jnp.float32),
        in_specs=[pl.BlockSpec(memory_space=pltpu.VMEM)] * 3,
        out_specs=pl.BlockSpec(memory_space=pltpu.VMEM),
        scratch_shapes=[
            pltpu.VMEM((len(sizes), 8, wide), jnp.float32),
            pltpu.VMEM((copies, 8, wide), jnp.float32),
            pltpu.SemaphoreType.DMA((copies,)),
            pltpu.SemaphoreType.DMA((copies,)),
        ],
        compiler_params=pltpu.CompilerParams(collective_id=1, has_side_effects=True),
        name="totals",
    )(sums, obs, gain)[:, 0]


def spread_kernel(
    nt,
    no,
    step,
    factor_ref,
    grid_ref,
    out_ref,
    stage,
    core_in,
    chip,
    far_in,
    near_grid,
    grid_sem,
    core_send,
    core_recv,
    far_send,
    far_recv,
):
    tm, core = lax.axis_index("tm"), lax.axis_index("obs")
    hours, columns = grid_ref.shape
    own = hours // (nt * no)
    pieces = columns // step

    def fetch(piece):
        span = pl.ds(pl.multiple_of(piece * step, step), step)
        return pltpu.make_async_copy(grid_ref.at[:, span], near_grid.at[piece], grid_sem.at[piece])

    def begin(piece, carry):
        fetch(piece).start()
        return carry

    lax.fori_loop(0, pieces, begin, 0)
    barrier = pltpu.get_barrier_semaphore()
    for other in range(1, no):
        pl.semaphore_signal(barrier, inc=1, device_id={"obs": lax.rem(core + other, no)}, device_id_type=MESH)
    for other in range(1, nt):
        pl.semaphore_signal(barrier, inc=1, device_id={"tm": lax.rem(tm + other, nt)}, device_id_type=MESH)
    pl.semaphore_wait(barrier, nt + no - 2)

    def core_copy(piece, other):
        target = lax.rem(core + other, no)
        return pltpu.make_async_remote_copy(
            src_ref=stage.at[piece, target],
            dst_ref=core_in.at[other - 1, piece],
            send_sem=core_send.at[other - 1, piece],
            recv_sem=core_recv.at[other - 1, piece],
            device_id={"obs": target},
            device_id_type=MESH,
        )

    def far_copy(piece, other):
        target = lax.rem(tm + other, nt)
        return pltpu.make_async_remote_copy(
            src_ref=chip.at[piece, target],
            dst_ref=far_in.at[other - 1, piece],
            send_sem=far_send.at[other - 1, piece],
            recv_sem=far_recv.at[other - 1, piece],
            device_id={"tm": target},
            device_id_type=MESH,
        )

    def pair(piece):
        total = stage[piece, core].astype(jnp.float32)
        for other in range(1, no):
            core_copy(piece, other).wait_recv()
            total = total + core_in[other - 1, piece].astype(jnp.float32)
        chip[piece] = total.astype(jnp.bfloat16).reshape(nt, own, step)
        for other in range(1, nt):
            far_copy(piece, other).start()

    def work(piece, carry):
        fetch(piece).wait()
        product = jnp.dot(factor_ref[...], near_grid[piece], preferred_element_type=jnp.float32)
        product = product.astype(jnp.bfloat16)
        for j in range(nt):
            for k in range(no):
                row = (j * no + k) * own
                stage[piece, k, j * own : (j + 1) * own, :] = product[row : row + own]
        for other in range(1, no):
            core_copy(piece, other).start()

        @pl.when(piece > 0)
        def _():
            pair(piece - 1)

        return carry

    lax.fori_loop(0, pieces, work, 0)
    pair(pieces - 1)

    def last(piece, carry):
        span = pl.ds(pl.multiple_of(piece * step, step), step)
        total = chip[piece, tm].astype(jnp.float32)
        for other in range(1, nt):
            far_copy(piece, other).wait_recv()
            total = total + far_in[other - 1, piece].astype(jnp.float32)
        out_ref[:, span] = total.astype(jnp.bfloat16)
        for other in range(1, no):
            core_copy(piece, other).wait_send()
        for other in range(1, nt):
            far_copy(piece, other).wait_send()
        return carry

    lax.fori_loop(0, pieces, last, 0)


def spread_of(factor, grid):
    nt, no = lax.axis_size("tm"), lax.axis_size("obs")
    hours, columns = grid.shape
    own = hours // (nt * no)
    step = chunk_of(columns, 256)
    pieces = columns // step
    far, near = max(nt - 1, 1), max(no - 1, 1)
    return pl.pallas_call(
        functools.partial(spread_kernel, nt, no, step),
        out_shape=jax.ShapeDtypeStruct((own, columns), jnp.bfloat16),
        in_specs=[pl.BlockSpec(memory_space=pltpu.VMEM), pl.BlockSpec(memory_space=pl.ANY)],
        out_specs=pl.BlockSpec(memory_space=pltpu.VMEM),
        scratch_shapes=[
            pltpu.VMEM((pieces, no, nt * own, step), jnp.bfloat16),
            pltpu.VMEM((near, pieces, nt * own, step), jnp.bfloat16),
            pltpu.VMEM((pieces, nt, own, step), jnp.bfloat16),
            pltpu.VMEM((far, pieces, own, step), jnp.bfloat16),
            pltpu.VMEM((pieces, hours, step), jnp.bfloat16),
            pltpu.SemaphoreType.DMA((pieces,)),
            pltpu.SemaphoreType.DMA((near, pieces)),
            pltpu.SemaphoreType.DMA((near, pieces)),
            pltpu.SemaphoreType.DMA((far, pieces)),
            pltpu.SemaphoreType.DMA((far, pieces)),
        ],
        compiler_params=pltpu.CompilerParams(
            collective_id=2, has_side_effects=True, vmem_limit_bytes=58 * 1024 * 1024
        ),
        name="spread",
    )(factor, grid)


def per_device(
    state,
    spatial_factor,
    time_factor,
    footprints,
    tile_obs,
    tile_block,
    tile_hour,
    tile_count,
    obs_weight,
):
    slots, lags, width = footprints.shape
    blocks = spatial_factor.shape[0] // width
    rows = -(-lags // ALIGN) * ALIGN + ALIGN
    own_live = (jnp.arange(slots, dtype=jnp.int32) < tile_count[0, 0]).astype(jnp.int32)
    table = jnp.stack([tile_obs[:, 0], tile_block[:, 0], tile_hour[:, 0], own_live])
    table = jnp.pad(table, ((0, 4), (0, 128 - slots)))
    tiles, factor, table = gathered(footprints, time_factor, table)
    tile_obs, tile_block, tile_hour, tile_live = [table[:, row, :slots].reshape(-1) for row in range(4)]
    full_state = lax.all_gather(state, ("tm", "obs"), axis=0, tiled=True)
    hours = factor.shape[0]
    count = tiles.shape[0]

    key = jnp.where(tile_live > 0, tile_block, blocks)
    number = jnp.arange(count, dtype=jnp.int32)
    before = (key[None, :] < key[:, None]) | ((key[None, :] == key[:, None]) & (number[None, :] < number[:, None]))
    rank = jnp.sum(before.astype(jnp.int32), axis=1)
    at_rank = (rank[None, :] == number[:, None]).astype(jnp.int32)
    order = jnp.sum(at_rank * number[None, :], axis=1)
    hour = jnp.sum(at_rank * tile_hour[None, :], axis=1)
    obs = jnp.sum(at_rank * tile_obs[None, :], axis=1)
    edges = jnp.arange(blocks + 1, dtype=jnp.int32)
    start = jnp.sum((key[None, :] < edges[:, None]).astype(jnp.int32), axis=1)
    live = start[blocks:]
    base = jnp.minimum(hour // ALIGN * ALIGN, hours - rows)
    shift = hour - base

    image = images(order, shift, start, tiles, spatial_factor, rows)
    sums = window_sums(base, live, factor, full_state, image)
    weight = weights_of(sums, obs, obs_weight, ("space", "tm", "obs"))
    spread = spread_of(factor, placed(base, live, weight, image, hours))
    return state.astype(jnp.float32) + spread.astype(jnp.float32)


def solution(mesh):
    return jax.shard_map(
        per_device,
        mesh=mesh,
        in_specs=(
            P(("groups", "tm", "obs"), "space"),
            P(("tm", "obs"), "space"),
            P("space", None),
            P(("groups", "space"), None, ("tm", "obs")),
            P(("groups", "space"), ("tm", "obs")),
            P(("groups", "space"), ("tm", "obs")),
            P(("groups", "space"), ("tm", "obs")),
            P(("groups", "space"), ("tm", "obs")),
            P("groups"),
        ),
        out_specs=P(("groups", "tm", "obs"), "space"),
        check_vma=False,
    )
```
